32 devices in a mesh: groups: 2 (over x), seq: 16 (over z, y, core).
Axes of the slice: x: 2, y: 2, z: 4, core: 2. Of those that a mesh axis runs over, the one named last changes fastest.
Arguments:
- hidden: bfloat16 [12288, 3072], P(('groups', 'seq')), parts along dimension 0, may hold values from -6 to 6
- query_rows: bfloat16 [12288, 1536], P(('groups', 'seq')), parts along dimension 0, may hold values from -200 to 200
- key_rows: bfloat16 [12288, 1536], P(('groups', 'seq')), parts along dimension 0, may hold values from -10 to 10
- value_rows: bfloat16 [12288, 1536], P(('groups', 'seq')), parts along dimension 0, may hold values from -6 to 6
- out_weight: bfloat16 [1536, 3072], replicated, may hold values from -1.25 to 1.25
- masked_tiles: int32 [24], P('groups'), parts along dimension 0, may hold values from 0 to 47, as said below
Outputs:
- painted: bfloat16 [12288, 3072], P(('groups', 'seq')), parts along dimension 0
The draws below stay inside these ranges and needn't reach their ends.
There are 2 independent parts, one for each index of `groups`. The reference program is written for one: setup_inputs(seed, part) draws one part's arguments, and reference() takes and returns one part's arrays. A program takes and returns all parts, laid end to end along the dimension named above; an argument that names none is the same for every part. Nothing has to cross between parts.
Inputs may be any that keep to these rules, and one draw needn't show every extreme that they name: `masked_tiles`: 12 distinct tile indices in increasing order; in every clip all 3 tiles of one index of seq (tiles d * 3 to (d + 1) * 3 - 1) are masked.
All inputs are finite; a program needn't handle non-finite values.
Results may differ from the reference program's by a relative error of at most 0.0065.
Values may be sent and summed in bfloat16 or wider, within the bound.
A program may use at most 128 MiB of HBM per device.

```python
import math
import jax
import jax.numpy as jnp
from jax import lax

D = 3072
HEADS = 24
HEAD_DIM = 64
TILE = 128
TILES_DEV = 3
AW = 1536
TILES = 48
TOKENS = 6144
MASKED = 12


def shared_normal(key):
    return jnp.clip(jax.random.normal(key, (TOKENS, AW), jnp.float32), -5.0, 5.0)


def draw_query_rows(key, part):
    key = jax.random.fold_in(key, 5)
    values = 1.41 * jnp.clip(jax.random.normal(key, (TOKENS, AW), jnp.float32), -5.0, 5.0)
    return values.astype(jnp.bfloat16)


def draw_key_rows(key, part):
    base = key
    common = 1.41 * shared_normal(base)
    values = common
    return values.astype(jnp.bfloat16)


def draw_masked_tiles(key, part):
    key = jax.random.fold_in(key, 3)
    first_key, second_key = jax.random.split(key)
    full_device = jax.random.randint(first_key, (), 0, TILES // TILES_DEV)
    order = jax.random.permutation(second_key, TILES).astype(jnp.int32) + TILES_DEV
    tile_ids = jnp.arange(TILES, dtype=jnp.int32)
    inside = tile_ids // TILES_DEV == full_device
    score = jnp.where(inside, tile_ids % TILES_DEV, order)
    picked = jnp.argsort(score, stable=True)[:MASKED]
    return jnp.sort(picked).astype(jnp.int32)


def shard_levels(stream_key, dims, cuts, least, top_value):
    def one(axis_at, shards_of):
        draws = jax.random.uniform(jax.random.fold_in(jax.random.fold_in(stream_key, 6), axis_at), (shards_of,), jnp.float32, least / len(cuts), top_value / len(cuts))
        return jnp.repeat(jnp.exp(draws), dims[axis_at] // shards_of).reshape((-1,) + (1,) * (len(dims) - axis_at - 1))

    gain = one(*cuts[0])
    for cut in cuts[1:]:
        gain = gain * one(*cut)
    return gain


def bell_draw(stream_key, extent, scale, limit, pieces=(), kind=jnp.bfloat16):
    result = jax.random.normal(stream_key, extent, jnp.float32) * scale
    if len(pieces) > 0:
        result = shard_levels(stream_key, extent, pieces, -0.22, 0.18) * result
    return jnp.clip(result, min=-limit, max=limit).astype(kind)


def setup_inputs(seed: int = 0, part: int = 0) -> dict:
    seeds = jax.random.split(jax.random.key(seed), 7)
    own_keys = jax.random.split(jax.random.fold_in(seeds[6], part), 7)
    hidden = bell_draw(own_keys[0], (TOKENS, D), 1.0, 6.0, ((0, 16),))
    query_rows = draw_query_rows(jax.random.fold_in(jax.random.fold_in(seeds[6], part), 71), part)
    key_rows = draw_key_rows(jax.random.fold_in(jax.random.fold_in(seeds[6], part), 71), part)
    value_rows = bell_draw(own_keys[3], (TOKENS, AW), 1.0, 6.0, ((0, 16),))
    out_weight = bell_draw(seeds[4], (AW, D), (max(AW // 64, 1)) ** -0.5, 1.25)
    masked_tiles = draw_masked_tiles(jax.random.fold_in(jax.random.fold_in(seeds[6], part), 71), part)
    return dict(hidden=hidden, query_rows=query_rows, key_rows=key_rows, value_rows=value_rows, out_weight=out_weight, masked_tiles=masked_tiles)


def reference(hidden, query_rows, key_rows, value_rows, out_weight, masked_tiles):
    rows = (masked_tiles[:, None] * TILE + jnp.arange(TILE, dtype=jnp.int32)[None, :]).reshape(-1).astype(jnp.int32)
    queries = jnp.take(query_rows, rows, axis=0)
    keys_all = jnp.take(key_rows, rows, axis=0)
    values_all = jnp.take(value_rows, rows, axis=0)
    scale = 1.0 / math.sqrt(HEAD_DIM)

    def per_head(head_index):
        start = (head_index * HEAD_DIM).astype(jnp.int32)
        query_head = lax.dynamic_slice_in_dim(queries, start, HEAD_DIM, 1)
        key_head = lax.dynamic_slice_in_dim(keys_all, start, HEAD_DIM, 1)
        value_head = lax.dynamic_slice_in_dim(values_all, start, HEAD_DIM, 1)
        scores = jnp.dot(query_head, key_head.T, preferred_element_type=jnp.float32) * scale
        weights = jnp.exp(scores - lax.optimization_barrier(jnp.max(scores, axis=1, keepdims=True)))
        total = lax.optimization_barrier(jnp.sum(weights, axis=1, keepdims=True))
        summed = jnp.dot(weights.astype(jnp.bfloat16), value_head, preferred_element_type=jnp.float32)
        return summed / total
    stacked = lax.map(per_head, jnp.arange(HEADS, dtype=jnp.int32))
    attended = jnp.transpose(stacked, (1, 0, 2)).reshape(rows.shape[0], HEADS * HEAD_DIM).astype(jnp.bfloat16)
    residual = jnp.dot(attended, out_weight, preferred_element_type=jnp.float32).astype(jnp.bfloat16)
    painted = hidden.astype(jnp.float32).at[rows].add(residual.astype(jnp.float32))
    return painted.astype(jnp.bfloat16)
```

```python
import functools
import math

import jax
import jax.numpy as jnp
from jax import lax
from jax.experimental import pallas as pl
from jax.experimental.pallas import tpu as pltpu
from jax.sharding import PartitionSpec as P

HEADS = 24
TILE = 128
TILES_DEV = 3
LANES = 128
MESH = pl.DeviceIdType.MESH


def ring_device(place, chips, core):
    place = lax.rem(place + chips, chips)
    if chips == 8:
        chip = jnp.where(place < 4, 2 * place, 2 * (7 - place) + 1)
    else:
        chip = place
    return 2 * chip + core


def ring_place(device, chips):
    chip = device // 2
    if chips == 8:
        return jnp.where(lax.rem(chip, 2) == 0, chip // 2, 7 - chip // 2)
    return chip


def attend_kernel(n, own_ref, q_ref, o_ref, kv, qs, best, acc, hop_send, hop_recv, mate_send, mate_recv):
    device = lax.axis_index("seq")
    core = lax.rem(device, 2)
    chips = n // 2
    half = chips // 2
    place = ring_place(device, chips)
    sides = (ring_device(place + 1, chips, core), ring_device(place - 1, chips, core))
    mate = device + 1 - 2 * core
    rows = own_ref.shape[0]
    width = q_ref.shape[1]
    pairs = width // LANES

    barrier = pltpu.get_barrier_semaphore()
    for other in (*sides, mate):
        pl.semaphore_signal(barrier, inc=1, device_id={"seq": other}, device_id_type=MESH)
    pl.semaphore_wait(barrier, 3)

    def slot(step):
        return 0 if step == 0 else 2 * rows + (step - 1) * 4 * rows

    def region(step, side, start=0, size=rows):
        base = slot(step) + (2 * rows * side if step < half else 0) + start
        return pl.ds(pl.multiple_of(base + core * rows, 16), size)

    def hop(src, dst, step, side):
        copy = pltpu.make_async_remote_copy(
            src_ref=src, dst_ref=kv.at[dst], send_sem=hop_send.at[side, step], recv_sem=hop_recv.at[side, step],
            device_id={"seq": sides[side]}, device_id_type=MESH)
        copy.start()
        return copy

    def share(src, dst, step, side):
        copy = pltpu.make_async_remote_copy(
            src_ref=src, dst_ref=kv.at[dst], send_sem=mate_send.at[side, step], recv_sem=mate_recv.at[side, step],
            device_id={"seq": mate}, device_id_type=MESH)
        copy.start()
        return copy

    def compute(start, length, first):
        def one_pair(h, carry):
            columns = pl.ds(pl.multiple_of(h * LANES, LANES), LANES)
            value_columns = pl.ds(pl.multiple_of(width + h * LANES, LANES), LANES)
            keys = kv[start:start + length, columns]
            values = kv[start:start + length, value_columns]
            low = lax.broadcasted_iota(jnp.int32, (1, LANES), 1) < LANES // 2
            for odd in range(2):
                mine = low if odd == 0 else jnp.logical_not(low)
                value_one = jnp.where(mine, values, jnp.ones_like(values))
                scores = lax.dot_general(qs[h, odd], keys, (((1,), (1,)), ((), ())), preferred_element_type=jnp.float32)
                top = jnp.max(scores, axis=1, keepdims=True)
                if first:
                    weights = jnp.exp(scores - top)
                    acc[h, odd] = jnp.dot(weights.astype(jnp.bfloat16), value_one, preferred_element_type=jnp.float32)
                    best[h, odd] = top
                else:
                    old = best[h, odd]
                    new = jnp.maximum(old, top)
                    weights = jnp.exp(scores - new)
                    part = jnp.dot(weights.astype(jnp.bfloat16), value_one, preferred_element_type=jnp.float32)
                    acc[h, odd] = acc[h, odd] * jnp.exp(old - new) + part
                    best[h, odd] = new
            return carry

        lax.fori_loop(0, pairs, one_pair, 0)

    sent = []
    hops = [hop(own_ref, region(1, side), 1, side) for side in range(2)]
    mates = [share(own_ref, region(0, 0), 0, 0)]
    sent += hops + mates
    kv[region(0, 0), :] = own_ref[...]

    scale = 1.0 / math.sqrt(width // HEADS)

    def split_pair(h, carry):
        columns = pl.ds(pl.multiple_of(h * LANES, LANES), LANES)
        both = q_ref[:, columns].astype(jnp.float32) * scale
        low = lax.broadcasted_iota(jnp.int32, (1, LANES), 1) < LANES // 2
        qs[h, 0] = jnp.where(low, both, 0.0).astype(jnp.bfloat16)
        qs[h, 1] = jnp.where(low, 0.0, both).astype(jnp.bfloat16)
        return carry

    lax.fori_loop(0, pairs, split_pair, 0)

    for step in range(1, half + 1):
        for copy in hops:
            copy.wait_recv()
        new_mates = []
        if step < half:
            if step < half - 1:
                hops = [hop(kv.at[region(step, side)], region(step + 1, side), step + 1, side) for side in range(2)]
            else:
                hops = [
                    hop(kv.at[region(step, side, side * rows // 2, rows // 2)],
                        region(step + 1, side, side * rows // 2, rows // 2), step + 1, side)
                    for side in range(2)
                ]
            sent += hops
            new_mates = [share(kv.at[region(step, side)], region(step, side), step, side) for side in range(2)]
        else:
            new_mates = [share(kv.at[region(step, 0)], region(step, 0), step, 0)]
        sent += new_mates
        for copy in mates:
            copy.wait_recv()
        mates = new_mates
        compute(slot(step - 1), slot(step) - slot(step - 1), step == 1)
    for copy in mates:
        copy.wait_recv()
    compute(slot(half), 2 * rows, False)

    def finish(h, carry):
        columns = pl.ds(pl.multiple_of(h * LANES, LANES), LANES)
        low = lax.broadcasted_iota(jnp.int32, (1, LANES), 1) < LANES // 2
        even, odd = acc[h, 0], acc[h, 1]
        total_even = even[:, LANES // 2:LANES // 2 + 1]
        total_odd = odd[:, 0:1]
        o_ref[:, columns] = jnp.where(low, even / total_even, odd / total_odd).astype(jnp.bfloat16)
        return carry

    lax.fori_loop(0, pairs, finish, 0)
    for copy in sent:
        copy.wait_send()


def attend(own, queries, n):
    rows, width = queries.shape
    pairs = width // LANES
    half = n // 4
    vmem = pl.BlockSpec(memory_space=pltpu.VMEM)
    return pl.pallas_call(
        functools.partial(attend_kernel, n),
        out_shape=jax.ShapeDtypeStruct((rows, width), jnp.bfloat16),
        in_specs=[vmem, vmem],
        out_specs=vmem,
        scratch_shapes=[
            pltpu.VMEM((own.shape[0] * n, 2 * width), jnp.bfloat16),
            pltpu.VMEM((pairs, 2, rows, LANES), jnp.bfloat16),
            pltpu.VMEM((pairs, 2, rows, 1), jnp.float32),
            pltpu.VMEM((pairs, 2, rows, LANES), jnp.float32),
            pltpu.SemaphoreType.DMA((2, half + 1)),
            pltpu.SemaphoreType.DMA((2, half + 1)),
            pltpu.SemaphoreType.DMA((2, half + 1)),
            pltpu.SemaphoreType.DMA((2, half + 1)),
        ],
        compiler_params=pltpu.CompilerParams(
            collective_id=0, has_side_effects=True, vmem_limit_bytes=52 * 1024 * 1024
        ),
    )(own, queries)


def body(hidden, query_rows, key_rows, value_rows, out_weight, masked_tiles):
    n = lax.axis_size("seq")
    device = lax.axis_index("seq")
    tokens, width = key_rows.shape
    both = jnp.concatenate([key_rows, value_rows], axis=1).reshape(TILES_DEV, TILE, 2 * width)
    got = lax.all_to_all(both, "seq", split_axis=1, concat_axis=0, tiled=True)
    own = jnp.take(got, masked_tiles, axis=0, mode="clip").reshape(-1, 2 * width)
    attended = attend(own, query_rows, n)
    here = device * TILES_DEV + jnp.arange(tokens, dtype=jnp.int32) // TILE
    masked = jnp.any(here[:, None] == masked_tiles[None, :], axis=1)
    residual = jnp.dot(attended, out_weight, preferred_element_type=jnp.float32).astype(jnp.bfloat16)
    residual = jnp.where(masked[:, None], residual, jnp.zeros_like(residual))
    painted = hidden.astype(jnp.float32) + residual.astype(jnp.float32)
    return painted.astype(jnp.bfloat16)


def solution(mesh):
    placed = (
        P(("groups", "seq"), None),
        P(("groups", "seq"), None),
        P(("groups", "seq"), None),
        P(("groups", "seq"), None),
        P(),
        P("groups"),
    )
    return jax.shard_map(
        body, mesh=mesh, in_specs=placed, out_specs=P(("groups", "seq"), None), check_vma=False
    )
```

```python
import functools
import math

import jax
import jax.numpy as jnp
from jax import lax
from jax.experimental import pallas as pl
from jax.experimental.pallas import tpu as pltpu
from jax.sharding import PartitionSpec as P

HEADS = 24
TILE = 128
TILES_DEV = 3
LANES = 128
HALF = 64
ONES = 16
MESH = pl.DeviceIdType.MESH


def ring_device(place, chips, core):
    place = lax.rem(place + chips, chips)
    if chips == 8:
        chip = jnp.where(place < 4, 2 * place, 2 * (7 - place) + 1)
    else:
        chip = place
    return 2 * chip + core


def ring_place(device, chips):
    chip = device // 2
    if chips == 8:
        return jnp.where(lax.rem(chip, 2) == 0, chip // 2, 7 - chip // 2)
    return chip


def attend_kernel(n, own_ref, q_ref, o_ref, kv, qs, best, acc, hop_send, hop_recv, mate_send, mate_recv):
    device = lax.axis_index("seq")
    core = lax.rem(device, 2)
    chips = n // 2
    half = chips // 2
    place = ring_place(device, chips)
    sides = (ring_device(place + 1, chips, core), ring_device(place - 1, chips, core))
    mate = device + 1 - 2 * core
    rows = own_ref.shape[0]
    queries, width = q_ref.shape
    pairs = width // LANES

    barrier = pltpu.get_barrier_semaphore()
    for other in (*sides, mate):
        pl.semaphore_signal(barrier, inc=1, device_id={"seq": other}, device_id_type=MESH)
    pl.semaphore_wait(barrier, 3)

    def slot(step):
        return 0 if step == 0 else 2 * rows + (step - 1) * 4 * rows

    def region(step, side, start=0, size=rows):
        base = slot(step) + (2 * rows * side if step < half else 0) + start
        return pl.ds(pl.multiple_of(base + core * rows, 16), size)

    def hop(src, dst, step, side):
        copy = pltpu.make_async_remote_copy(
            src_ref=src, dst_ref=kv.at[dst], send_sem=hop_send.at[side, step], recv_sem=hop_recv.at[side, step],
            device_id={"seq": sides[side]}, device_id_type=MESH)
        copy.start()
        return copy

    def share(src, dst, step, side):
        copy = pltpu.make_async_remote_copy(
            src_ref=src, dst_ref=kv.at[dst], send_sem=mate_send.at[side, step], recv_sem=mate_recv.at[side, step],
            device_id={"seq": mate}, device_id_type=MESH)
        copy.start()
        return copy

    def compute(start, length, first):
        def one_pair(h, carry):
            columns = pl.ds(pl.multiple_of(h * LANES, LANES), LANES)
            value_columns = pl.ds(pl.multiple_of(width + h * LANES, LANES), LANES)
            keys = kv[start:start + length, columns]
            values = jnp.transpose(kv[start:start + length, value_columns])
            ones = jnp.ones((ONES, length), jnp.bfloat16)
            both = jnp.dot(keys, qs[h], preferred_element_type=jnp.float32)
            for odd in range(2):
                mine = values[odd * HALF:(odd + 1) * HALF]
                value_one = jnp.concatenate([mine, ones], axis=0)
                scores = both[:, odd * queries:(odd + 1) * queries]
                top = jnp.max(scores, axis=0, keepdims=True)
                if first:
                    weights = jnp.exp(scores - top)
                    acc[h, odd] = jnp.dot(value_one, weights.astype(jnp.bfloat16), preferred_element_type=jnp.float32)
                    best[h, odd] = top
                else:
                    old = best[h, odd]
                    new = jnp.maximum(old, top)
                    weights = jnp.exp(scores - new)
                    part = jnp.dot(value_one, weights.astype(jnp.bfloat16), preferred_element_type=jnp.float32)
                    acc[h, odd] = acc[h, odd] * jnp.exp(old - new) + part
                    best[h, odd] = new
            return carry

        lax.fori_loop(0, pairs, one_pair, 0, unroll=2)

    sent = []
    hops = [hop(own_ref, region(1, side), 1, side) for side in range(2)]
    mates = [share(own_ref, region(0, 0), 0, 0)]
    sent += hops + mates
    kv[region(0, 0), :] = own_ref[...]

    scale = 1.0 / math.sqrt(width // HEADS)

    def split_pair(h, carry):
        columns = pl.ds(pl.multiple_of(h * LANES, LANES), LANES)
        both = jnp.transpose(q_ref[:, columns].astype(jnp.float32) * scale)
        low = lax.broadcasted_iota(jnp.int32, (LANES, 1), 0) < HALF
        qs[h, :, :queries] = jnp.where(low, both, 0.0).astype(jnp.bfloat16)
        qs[h, :, queries:] = jnp.where(low, 0.0, both).astype(jnp.bfloat16)
        return carry

    lax.fori_loop(0, pairs, split_pair, 0)

    for step in range(1, half + 1):
        for copy in hops:
            copy.wait_recv()
        new_mates = []
        if step < half:
            if step < half - 1:
                hops = [hop(kv.at[region(step, side)], region(step + 1, side), step + 1, side) for side in range(2)]
            else:
                hops = [
                    hop(kv.at[region(step, side, side * rows // 2, rows // 2)],
                        region(step + 1, side, side * rows // 2, rows // 2), step + 1, side)
                    for side in range(2)
                ]
            sent += hops
            new_mates = [share(kv.at[region(step, side)], region(step, side), step, side) for side in range(2)]
        else:
            new_mates = [share(kv.at[region(step, 0)], region(step, 0), step, 0)]
        sent += new_mates
        for copy in mates:
            copy.wait_recv()
        mates = new_mates
        compute(slot(step - 1), slot(step) - slot(step - 1), step == 1)
    for copy in mates:
        copy.wait_recv()
    compute(slot(half), 2 * rows, False)

    def finish(h, carry):
        columns = pl.ds(pl.multiple_of(h * LANES, LANES), LANES)
        done = [acc[h, odd, :HALF] / acc[h, odd, HALF:HALF + 1] for odd in range(2)]
        o_ref[:, columns] = jnp.transpose(jnp.concatenate(done, axis=0)).astype(jnp.bfloat16)
        return carry

    lax.fori_loop(0, pairs, finish, 0)
    for copy in sent:
        copy.wait_send()


def attend(own, queries, n):
    rows, width = queries.shape
    pairs = width // LANES
    half = n // 4
    vmem = pl.BlockSpec(memory_space=pltpu.VMEM)
    return pl.pallas_call(
        functools.partial(attend_kernel, n),
        out_shape=jax.ShapeDtypeStruct((rows, width), jnp.bfloat16),
        in_specs=[vmem, vmem],
        out_specs=vmem,
        scratch_shapes=[
            pltpu.VMEM((own.shape[0] * n, 2 * width), jnp.bfloat16),
            pltpu.VMEM((pairs, LANES, 2 * rows), jnp.bfloat16),
            pltpu.VMEM((pairs, 2, 1, rows), jnp.float32),
            pltpu.VMEM((pairs, 2, HALF + ONES, rows), jnp.float32),
            pltpu.SemaphoreType.DMA((2, half + 1)),
            pltpu.SemaphoreType.DMA((2, half + 1)),
            pltpu.SemaphoreType.DMA((2, half + 1)),
            pltpu.SemaphoreType.DMA((2, half + 1)),
        ],
        compiler_params=pltpu.CompilerParams(
            collective_id=0, has_side_effects=True, vmem_limit_bytes=52 * 1024 * 1024
        ),
    )(own, queries)


def body(hidden, query_rows, key_rows, value_rows, out_weight, masked_tiles):
    n = lax.axis_size("seq")
    device = lax.axis_index("seq")
    tokens, width = key_rows.shape
    both = jnp.concatenate([key_rows, value_rows], axis=1).reshape(TILES_DEV, TILE, 2 * width)
    got = lax.all_to_all(both, "seq", split_axis=1, concat_axis=0, tiled=True)
    own = jnp.take(got, masked_tiles, axis=0, mode="clip").reshape(-1, 2 * width)
    attended = attend(own, query_rows, n)
    here = device * TILES_DEV + jnp.arange(tokens, dtype=jnp.int32) // TILE
    masked = jnp.any(here[:, None] == masked_tiles[None, :], axis=1)
    residual = jnp.dot(attended, out_weight, preferred_element_type=jnp.float32).astype(jnp.bfloat16)
    residual = jnp.where(masked[:, None], residual, jnp.zeros_like(residual))
    painted = hidden.astype(jnp.float32) + residual.astype(jnp.float32)
    return painted.astype(jnp.bfloat16)


def solution(mesh):
    placed = (
        P(("groups", "seq"), None),
        P(("groups", "seq"), None),
        P(("groups", "seq"), None),
        P(("groups", "seq"), None),
        P(),
        P("groups"),
    )
    return jax.shard_map(
        body, mesh=mesh, in_specs=placed, out_specs=P(("groups", "seq"), None), check_vma=False
    )
```

```python
import functools
import math

import jax
import jax.numpy as jnp
from jax import lax
from jax.experimental import pallas as pl
from jax.experimental.pallas import tpu as pltpu
from jax.sharding import PartitionSpec as P

HEADS = 24
TILE = 128
TILES_DEV = 3
LANES = 128
HALF = 64
ONES = 16
MESH = pl.DeviceIdType.MESH


def ring_device(place, chips, core):
    place = lax.rem(place + chips, chips)
    if chips == 8:
        chip = jnp.where(place < 4, 2 * place, 2 * (7 - place) + 1)
    else:
        chip = place
    return 2 * chip + core


def ring_place(device, chips):
    chip = device // 2
    if chips == 8:
        return jnp.where(lax.rem(chip, 2) == 0, chip // 2, 7 - chip // 2)
    return chip


def attend_kernel(n, tiles_ref, dealt_ref, q_ref, o_ref, got, kv, qs, best, acc, sems):
    deal_send, deal_recv, hop_send, hop_recv, mate_send, mate_recv = sems
    device = lax.axis_index("seq")
    core = lax.rem(device, 2)
    chips = n // 2
    half = chips // 2
    place = ring_place(device, chips)
    sides = (ring_device(place + 1, chips, core), ring_device(place - 1, chips, core))
    mate = device + 1 - 2 * core
    queries, width = q_ref.shape
    pairs = width // LANES
    share_rows = dealt_ref.shape[3]
    rows = kv.shape[1] // chips
    part = rows // 2

    barrier = pltpu.get_barrier_semaphore()
    for away in range(1, n):
        other = lax.rem(device + away, n)
        pl.semaphore_signal(barrier, inc=1, device_id={"seq": other}, device_id_type=MESH)
    pl.semaphore_wait(barrier, n - 1)

    def slot(step):
        return 0 if step == 0 else rows + (step - 1) * 2 * rows

    def region(step, side, chunk):
        base = slot(step) + (rows * side if 0 < step < half else 0)
        return kv.at[core, pl.ds(base + chunk * part, part)]

    def remote(src, dst, send, recv, target):
        copy = pltpu.make_async_remote_copy(
            src_ref=src, dst_ref=dst, send_sem=send, recv_sem=recv,
            device_id={"seq": target}, device_id_type=MESH)
        copy.start()
        return copy

    def hop(step, side, chunk):
        return remote(region(step - 1, side, chunk), region(step, side, chunk), hop_send.at[side, step, chunk],
                      hop_recv.at[side, step, chunk], sides[side])

    def share(step, side, chunk):
        block = region(step, side, chunk)
        return remote(block, block, mate_send.at[side, step, chunk], mate_recv.at[side, step, chunk], mate)

    def compute(start, length, first, low_pair, high_pair):
        def one_pair(h, carry):
            columns = pl.ds(pl.multiple_of(h * LANES, LANES), LANES)
            keys = kv[0, start:start + length, columns]
            values = jnp.transpose(kv[1, start:start + length, columns])
            ones = jnp.ones((ONES, length), jnp.bfloat16)
            both = jnp.dot(keys, qs[h], preferred_element_type=jnp.float32)
            for odd in range(2):
                mine = values[odd * HALF:(odd + 1) * HALF]
                value_one = jnp.concatenate([mine, ones], axis=0)
                scores = both[:, odd * queries:(odd + 1) * queries]
                top = jnp.max(scores, axis=0, keepdims=True)
                if first:
                    weights = jnp.exp(scores - top)
                    acc[h, odd] = jnp.dot(value_one, weights.astype(jnp.bfloat16), preferred_element_type=jnp.float32)
                    best[h, odd] = top
                else:
                    old = best[h, odd]
                    new = jnp.maximum(old, top)
                    weights = jnp.exp(scores - new)
                    more = jnp.dot(value_one, weights.astype(jnp.bfloat16), preferred_element_type=jnp.float32)
                    acc[h, odd] = acc[h, odd] * jnp.exp(old - new) + more
                    best[h, odd] = new
            return carry

        lax.fori_loop(low_pair, high_pair, one_pair, 0, unroll=2)

    def landing(source):
        return got.at[pl.ds(TILES_DEV * source, TILES_DEV)]

    sent = []
    for away in range(n - 1, 0, -1):
        other = lax.rem(device + away, n)
        sent.append(remote(dealt_ref.at[lax.rem(other, 2), other // 2], landing(device), deal_send.at[away],
                           deal_recv.at[away], other))
    local = pltpu.make_async_copy(dealt_ref.at[core, device // 2], landing(device), deal_send.at[0])
    local.start()

    scale = 1.0 / math.sqrt(width // HEADS)

    def split_pair(h, carry):
        columns = pl.ds(pl.multiple_of(h * LANES, LANES), LANES)
        both = jnp.transpose(q_ref[:, columns].astype(jnp.float32) * scale)
        low = lax.broadcasted_iota(jnp.int32, (LANES, 1), 0) < HALF
        qs[h, :, :queries] = jnp.where(low, both, 0.0).astype(jnp.bfloat16)
        qs[h, :, queries:] = jnp.where(low, 0.0, both).astype(jnp.bfloat16)
        return carry

    lax.fori_loop(0, pairs, split_pair, 0)

    local.wait()
    for copy in sent:
        copy.wait_recv()
    for index in range(tiles_ref.shape[0]):
        kv[core, index * share_rows:(index + 1) * share_rows] = got[tiles_ref[index]]

    hops = [[hop(1, side, chunk) for side in range(2)] for chunk in range(2)]
    mates = [share(0, 0, chunk) for chunk in range(2)]
    sent += hops[0] + hops[1] + mates
    for step in range(1, half + 1):
        new_hops, new_mates = [[], []], []
        for chunk in range(2):
            for copy in hops[chunk]:
                copy.wait_recv()
            if step < half - 1:
                new_hops[chunk] = [hop(step + 1, side, chunk) for side in range(2)]
            elif step == half - 1:
                new_hops[chunk] = [hop(half, chunk, chunk)]
            shared = [share(step, side, chunk) for side in range(2 if step < half else 1)]
            sent += new_hops[chunk] + shared
            new_mates += shared
            if chunk == 0:
                for copy in mates:
                    copy.wait_recv()
            compute(slot(step - 1), slot(step) - slot(step - 1), step == 1, chunk * (pairs // 2), (chunk + 1) * (pairs // 2))
        hops, mates = new_hops, new_mates
    for copy in mates:
        copy.wait_recv()
    compute(slot(half), rows, False, 0, pairs)

    def finish(h, carry):
        columns = pl.ds(pl.multiple_of(h * LANES, LANES), LANES)
        done = [acc[h, odd, :HALF] / acc[h, odd, HALF:HALF + 1] for odd in range(2)]
        o_ref[:, columns] = jnp.transpose(jnp.concatenate(done, axis=0)).astype(jnp.bfloat16)
        return carry

    lax.fori_loop(0, pairs, finish, 0)
    for copy in sent:
        copy.wait_send()


def attend(dealt, queries, tiles, n):
    rows, width = queries.shape
    pairs = width // LANES
    half = n // 4
    vmem = pl.BlockSpec(memory_space=pltpu.VMEM)
    share_rows = dealt.shape[3]
    hop_sems = pltpu.SemaphoreType.DMA((2, half + 1, 2))
    return pl.pallas_call(
        functools.partial(attend_kernel, n),
        out_shape=jax.ShapeDtypeStruct((rows, width), jnp.bfloat16),
        in_specs=[pl.BlockSpec(memory_space=pltpu.SMEM), pl.BlockSpec(memory_space=pl.ANY), vmem],
        out_specs=vmem,
        scratch_shapes=[
            pltpu.VMEM((n * TILES_DEV, share_rows, width), jnp.bfloat16),
            pltpu.VMEM((2, tiles.shape[0] * TILE, width), jnp.bfloat16),
            pltpu.VMEM((pairs, LANES, 2 * rows), jnp.bfloat16),
            pltpu.VMEM((pairs, 2, 1, rows), jnp.float32),
            pltpu.VMEM((pairs, 2, HALF + ONES, rows), jnp.float32),
            [pltpu.SemaphoreType.DMA((n,)), pltpu.SemaphoreType.DMA((n,)), hop_sems, hop_sems, hop_sems, hop_sems],
        ],
        compiler_params=pltpu.CompilerParams(
            collective_id=0, has_side_effects=True, vmem_limit_bytes=52 * 1024 * 1024
        ),
    )(tiles, dealt, queries)


def body(hidden, query_rows, key_rows, value_rows, out_weight, masked_tiles):
    n = lax.axis_size("seq")
    device = lax.axis_index("seq")
    tokens, width = key_rows.shape

    def by_chip(field):
        return jnp.transpose(field.reshape(TILES_DEV, n // 2, 2 * TILE // n, width), (1, 0, 2, 3))

    dealt = jnp.stack([by_chip(key_rows), by_chip(value_rows)])
    attended = attend(dealt, query_rows, masked_tiles, n)
    here = device * TILES_DEV + jnp.arange(tokens, dtype=jnp.int32) // TILE
    masked = jnp.any(here[:, None] == masked_tiles[None, :], axis=1)
    residual = jnp.dot(attended, out_weight, preferred_element_type=jnp.float32).astype(jnp.bfloat16)
    residual = jnp.where(masked[:, None], residual, jnp.zeros_like(residual))
    painted = hidden.astype(jnp.float32) + residual.astype(jnp.float32)
    return painted.astype(jnp.bfloat16)


def solution(mesh):
    placed = (
        P(("groups", "seq"), None),
        P(("groups", "seq"), None),
        P(("groups", "seq"), None),
        P(("groups", "seq"), None),
        P(),
        P("groups"),
    )
    return jax.shard_map(
        body, mesh=mesh, in_specs=placed, out_specs=P(("groups", "seq"), None), check_vma=False
    )
```

```python
import functools
import math

import jax
import jax.numpy as jnp
from jax import lax
from jax.experimental import pallas as pl
from jax.experimental.pallas import tpu as pltpu
from jax.sharding import PartitionSpec as P

HEADS = 24
TILE = 128
TILES_DEV = 3
LANES = 128
HALF = 64
ONES = 16
MESH = pl.DeviceIdType.MESH


def ring_device(place, chips, core):
    place = lax.rem(place + chips, chips)
    if chips == 8:
        chip = jnp.where(place < 4, 2 * place, 2 * (7 - place) + 1)
    else:
        chip = place
    return 2 * chip + core


def ring_place(device, chips):
    chip = device // 2
    if chips == 8:
        return jnp.where(lax.rem(chip, 2) == 0, chip // 2, 7 - chip // 2)
    return chip


def attend_kernel(n, tiles_ref, dealt_ref, q_ref, o_ref, got, kv, qs, best, acc, sems):
    deal_send, deal_recv, hop_send, hop_recv, mate_send, mate_recv = sems
    device = lax.axis_index("seq")
    core = lax.rem(device, 2)
    chips = n // 2
    half = chips // 2
    place = ring_place(device, chips)
    sides = (ring_device(place + 1, chips, core), ring_device(place - 1, chips, core))
    mate = device + 1 - 2 * core
    queries, width = q_ref.shape
    pairs = width // LANES
    share_rows = dealt_ref.shape[3]
    rows = kv.shape[1] // chips
    part = rows // 2

    barrier = pltpu.get_barrier_semaphore()
    for away in range(1, n):
        other = lax.rem(device + away, n)
        pl.semaphore_signal(barrier, inc=1, device_id={"seq": other}, device_id_type=MESH)
    pl.semaphore_wait(barrier, n - 1)

    def slot(step):
        return 0 if step == 0 else rows + (step - 1) * 2 * rows

    columns_of = [pl.ds(chunk * (width // 2), width // 2) for chunk in range(2)]

    def region(step, side, chunk, last=False):
        base = slot(step) + (rows * side if 0 < step < half else 0)
        start, size = (side * part, part) if last else (0, rows)
        return kv.at[core, pl.ds(base + start, size), columns_of[chunk]]

    def remote(src, dst, send, recv, target):
        copy = pltpu.make_async_remote_copy(
            src_ref=src, dst_ref=dst, send_sem=send, recv_sem=recv,
            device_id={"seq": target}, device_id_type=MESH)
        copy.start()
        return copy

    def hop(step, side, chunk):
        last = step == half
        return remote(region(step - 1, side, chunk, last), region(step, side, chunk, last), hop_send.at[side, step, chunk],
                      hop_recv.at[side, step, chunk], sides[side])

    def share(step, side, chunk):
        block = region(step, side, chunk)
        return remote(block, block, mate_send.at[side, step, chunk], mate_recv.at[side, step, chunk], mate)

    def compute(start, length, first, low_pair, high_pair):
        def one_pair(h, carry):
            columns = pl.ds(pl.multiple_of(h * LANES, LANES), LANES)
            keys = kv[0, start:start + length, columns]
            values = jnp.transpose(kv[1, start:start + length, columns])
            ones = jnp.ones((ONES, length), jnp.bfloat16)
            both = jnp.dot(keys, qs[h], preferred_element_type=jnp.float32)
            for odd in range(2):
                mine = values[odd * HALF:(odd + 1) * HALF]
                value_one = jnp.concatenate([mine, ones], axis=0)
                scores = both[:, odd * queries:(odd + 1) * queries]
                top = jnp.max(scores, axis=0, keepdims=True)
                if first:
                    weights = jnp.exp(scores - top)
                    acc[h, odd] = jnp.dot(value_one, weights.astype(jnp.bfloat16), preferred_element_type=jnp.float32)
                    best[h, odd] = top
                else:
                    old = best[h, odd]
                    new = jnp.maximum(old, top)
                    weights = jnp.exp(scores - new)
                    more = jnp.dot(value_one, weights.astype(jnp.bfloat16), preferred_element_type=jnp.float32)
                    acc[h, odd] = acc[h, odd] * jnp.exp(old - new) + more
                    best[h, odd] = new
            return carry

        lax.fori_loop(low_pair, high_pair, one_pair, 0, unroll=2)

    def landing(source, chunk):
        return got[chunk].at[pl.ds(TILES_DEV * source, TILES_DEV)]

    dealt, local = [[], []], []
    for chunk in range(2):
        for away in range(n - 1, 0, -1):
            other = lax.rem(device + away, n)
            source = dealt_ref.at[lax.rem(other, 2), other // 2, :, :, columns_of[chunk]]
            dealt[chunk].append(remote(source, landing(device, chunk), deal_send.at[chunk, away],
                                       deal_recv.at[chunk, away], other))
        source = dealt_ref.at[core, device // 2, :, :, columns_of[chunk]]
        local.append(pltpu.make_async_copy(source, landing(device, chunk), deal_send.at[chunk, 0]))
        local[chunk].start()
    sent = dealt[0] + dealt[1]

    scale = 1.0 / math.sqrt(width // HEADS)

    def split_pair(h, carry):
        columns = pl.ds(pl.multiple_of(h * LANES, LANES), LANES)
        both = jnp.transpose(q_ref[:, columns].astype(jnp.float32) * scale)
        low = lax.broadcasted_iota(jnp.int32, (LANES, 1), 0) < HALF
        qs[h, :, :queries] = jnp.where(low, both, 0.0).astype(jnp.bfloat16)
        qs[h, :, queries:] = jnp.where(low, 0.0, both).astype(jnp.bfloat16)
        return carry

    lax.fori_loop(0, pairs, split_pair, 0)

    hops, mates = [[], []], [[], []]
    skew = 2
    for time in range(half + 2 + skew):
        for chunk in range(2):
            step = time - skew * chunk
            if step < 0 or step > half + 1:
                continue
            if step == 0:
                local[chunk].wait()
                for copy in dealt[chunk]:
                    copy.wait_recv()
                for index in range(tiles_ref.shape[0]):
                    picked = got[chunk][tiles_ref[index]]
                    kv[core, index * share_rows:(index + 1) * share_rows, columns_of[chunk]] = picked
                hops[chunk] = [hop(1, side, chunk) for side in range(2)]
                mates[chunk] = [share(0, 0, chunk)]
                sent += hops[chunk] + mates[chunk]
                continue
            for copy in hops[chunk]:
                copy.wait_recv()
            hops[chunk] = [hop(step + 1, side, chunk) for side in range(2)] if step < half else []
            shared = [share(step, side, chunk) for side in range(2 if step < half else 1)] if step <= half else []
            sent += hops[chunk] + shared
            for copy in mates[chunk]:
                copy.wait_recv()
            mates[chunk] = shared
            length = 2 * rows if 0 < step - 1 < half else rows
            compute(slot(step - 1), length, step == 1, chunk * (pairs // 2), (chunk + 1) * (pairs // 2))

    def finish(h, carry):
        columns = pl.ds(pl.multiple_of(h * LANES, LANES), LANES)
        done = [acc[h, odd, :HALF] / acc[h, odd, HALF:HALF + 1] for odd in range(2)]
        o_ref[:, columns] = jnp.transpose(jnp.concatenate(done, axis=0)).astype(jnp.bfloat16)
        return carry

    lax.fori_loop(0, pairs, finish, 0)
    for copy in sent:
        copy.wait_send()


def attend(dealt, queries, tiles, n):
    rows, width = queries.shape
    pairs = width // LANES
    half = n // 4
    vmem = pl.BlockSpec(memory_space=pltpu.VMEM)
    share_rows = dealt.shape[3]
    hop_sems = pltpu.SemaphoreType.DMA((2, half + 1, 2))
    return pl.pallas_call(
        functools.partial(attend_kernel, n),
        out_shape=jax.ShapeDtypeStruct((rows, width), jnp.bfloat16),
        in_specs=[pl.BlockSpec(memory_space=pltpu.SMEM), pl.BlockSpec(memory_space=pl.ANY), vmem],
        out_specs=vmem,
        scratch_shapes=[
            [pltpu.VMEM((n * TILES_DEV, share_rows, width // 2), jnp.bfloat16)] * 2,
            pltpu.VMEM((2, tiles.shape[0] * TILE, width), jnp.bfloat16),
            pltpu.VMEM((pairs, LANES, 2 * rows), jnp.bfloat16),
            pltpu.VMEM((pairs, 2, 1, rows), jnp.float32),
            pltpu.VMEM((pairs, 2, HALF + ONES, rows), jnp.float32),
            [pltpu.SemaphoreType.DMA((2, n)), pltpu.SemaphoreType.DMA((2, n)), hop_sems, hop_sems, hop_sems, hop_sems],
        ],
        compiler_params=pltpu.CompilerParams(
            collective_id=0, has_side_effects=True, vmem_limit_bytes=52 * 1024 * 1024
        ),
    )(tiles, dealt, queries)


def body(hidden, query_rows, key_rows, value_rows, out_weight, masked_tiles):
    n = lax.axis_size("seq")
    device = lax.axis_index("seq")
    tokens, width = key_rows.shape

    def by_chip(field):
        return jnp.transpose(field.reshape(TILES_DEV, n // 2, 2 * TILE // n, width), (1, 0, 2, 3))

    dealt = jnp.stack([by_chip(key_rows), by_chip(value_rows)])
    attended = attend(dealt, query_rows, masked_tiles, n)
    here = device * TILES_DEV + jnp.arange(tokens, dtype=jnp.int32) // TILE
    masked = jnp.any(here[:, None] == masked_tiles[None, :], axis=1)
    residual = jnp.dot(attended, out_weight, preferred_element_type=jnp.float32).astype(jnp.bfloat16)
    residual = jnp.where(masked[:, None], residual, jnp.zeros_like(residual))
    painted = hidden.astype(jnp.float32) + residual.astype(jnp.float32)
    return painted.astype(jnp.bfloat16)


def solution(mesh):
    placed = (
        P(("groups", "seq"), None),
        P(("groups", "seq"), None),
        P(("groups", "seq"), None),
        P(("groups", "seq"), None),
        P(),
        P("groups"),
    )
    return jax.shard_map(
        body, mesh=mesh, in_specs=placed, out_specs=P(("groups", "seq"), None), check_vma=False
    )
```

```python
import functools
import math

import jax
import jax.numpy as jnp
from jax import lax
from jax.experimental import pallas as pl
from jax.experimental.pallas import tpu as pltpu
from jax.sharding import PartitionSpec as P

HEADS = 24
TILE = 128
TILES_DEV = 3
LANES = 128
HALF = 64
ONES = 16
MESH = pl.DeviceIdType.MESH


def ring_device(place, chips, core):
    place = lax.rem(place + chips, chips)
    if chips == 8:
        chip = jnp.where(place < 4, 2 * place, 2 * (7 - place) + 1)
    else:
        chip = place
    return 2 * chip + core


def ring_place(device, chips):
    chip = device // 2
    if chips == 8:
        return jnp.where(lax.rem(chip, 2) == 0, chip // 2, 7 - chip // 2)
    return chip


def attend_kernel(n, tiles_ref, keys_ref, values_ref, q_ref, o_ref, got, kv, qs, best, acc, sems):
    deal_send, deal_recv, hop_send, hop_recv, mate_send, mate_recv = sems
    device = lax.axis_index("seq")
    core = lax.rem(device, 2)
    chips = n // 2
    half = chips // 2
    place = ring_place(device, chips)
    sides = (ring_device(place + 1, chips, core), ring_device(place - 1, chips, core))
    mate = device + 1 - 2 * core
    queries, width = q_ref.shape
    pairs = width // LANES
    share_rows = keys_ref.shape[2]
    rows = kv.shape[1] // chips
    part = rows // 2

    barrier = pltpu.get_barrier_semaphore()
    for away in range(1, n):
        other = lax.rem(device + away, n)
        pl.semaphore_signal(barrier, inc=1, device_id={"seq": other}, device_id_type=MESH)
    pl.semaphore_wait(barrier, n - 1)

    def slot(step):
        return 0 if step == 0 else rows + (step - 1) * 2 * rows

    columns_of = [pl.ds(chunk * (width // 2), width // 2) for chunk in range(2)]

    def region(step, side, chunk, last=False):
        base = slot(step) + (rows * side if 0 < step < half else 0)
        start, size = (side * part, part) if last else (0, rows)
        return kv.at[core, pl.ds(base + start, size), columns_of[chunk]]

    def remote(src, dst, send, recv, target):
        copy = pltpu.make_async_remote_copy(
            src_ref=src, dst_ref=dst, send_sem=send, recv_sem=recv,
            device_id={"seq": target}, device_id_type=MESH)
        copy.start()
        return copy

    def hop(step, side, chunk):
        last = step == half
        return remote(region(step - 1, side, chunk, last), region(step, side, chunk, last), hop_send.at[side, step, chunk],
                      hop_recv.at[side, step, chunk], sides[side])

    def share(step, side, chunk):
        block = region(step, side, chunk)
        return remote(block, block, mate_send.at[side, step, chunk], mate_recv.at[side, step, chunk], mate)

    def compute(start, length, first, low_pair, high_pair):
        def one_pair(h, carry):
            columns = pl.ds(pl.multiple_of(h * LANES, LANES), LANES)
            keys = kv[0, start:start + length, columns]
            values = jnp.transpose(kv[1, start:start + length, columns])
            ones = jnp.ones((ONES, length), jnp.bfloat16)
            both = jnp.dot(keys, qs[h], preferred_element_type=jnp.float32)
            for odd in range(2):
                mine = values[odd * HALF:(odd + 1) * HALF]
                value_one = jnp.concatenate([mine, ones], axis=0)
                scores = both[:, odd * queries:(odd + 1) * queries]
                top = jnp.max(scores, axis=0, keepdims=True)
                if first:
                    weights = jnp.exp(scores - top)
                    acc[h, odd] = jnp.dot(value_one, weights.astype(jnp.bfloat16), preferred_element_type=jnp.float32)
                    best[h, odd] = top
                else:
                    old = best[h, odd]
                    new = jnp.maximum(old, top)
                    weights = jnp.exp(scores - new)
                    more = jnp.dot(value_one, weights.astype(jnp.bfloat16), preferred_element_type=jnp.float32)
                    acc[h, odd] = acc[h, odd] * jnp.exp(old - new) + more
                    best[h, odd] = new
            return carry

        lax.fori_loop(low_pair, high_pair, one_pair, 0, unroll=2)

    def landing(source, chunk):
        return got[chunk].at[pl.ds(TILES_DEV * source, TILES_DEV)]

    chip = device // 2
    fields = (keys_ref, values_ref)
    sent, arrivals, local = [], [[], []], []

    def to_mate(chunk, kept):
        source = fields[1 - kept].at[:, chip, :, columns_of[chunk]]
        return pltpu.make_async_remote_copy(
            src_ref=source, dst_ref=landing(device, chunk), send_sem=deal_send.at[chunk, 1],
            recv_sem=deal_recv.at[chunk, 1], device_id={"seq": mate}, device_id_type=MESH)

    def to_self(chunk, kept):
        source = fields[kept].at[:, chip, :, columns_of[chunk]]
        return pltpu.make_async_copy(source, landing(device, chunk), deal_send.at[chunk, 0])

    def deal(chunk):
        for away in range(chips - 1, 0, -1):
            other = lax.rem(chip + away, chips)
            for wanted in range(2):
                source = fields[wanted].at[:, other, :, columns_of[chunk]]
                send = deal_send.at[chunk, 2 * away + wanted]
                sent.append(remote(source, landing(device, chunk), send, deal_recv.at[chunk, 2 * away + core],
                                   2 * other + wanted))
                arrivals[chunk].append(pltpu.make_async_remote_copy(
                    src_ref=source, dst_ref=landing(device, chunk), send_sem=send,
                    recv_sem=deal_recv.at[chunk, 2 * away + wanted],
                    device_id={"seq": 2 * other + wanted}, device_id_type=MESH))
        for kept in range(2):
            @pl.when(core == kept)
            def _():
                to_mate(chunk, kept).start()
                to_self(chunk, kept).start()
        arrivals[chunk].append(to_mate(chunk, 0))
        sent.append(arrivals[chunk][-1])
        local.append(to_self(chunk, 0))

    deal(0)
    deal(1)

    scale = 1.0 / math.sqrt(width // HEADS)

    def split_pair(h, carry):
        columns = pl.ds(pl.multiple_of(h * LANES, LANES), LANES)
        both = jnp.transpose(q_ref[:, columns].astype(jnp.float32) * scale)
        low = lax.broadcasted_iota(jnp.int32, (LANES, 1), 0) < HALF
        qs[h, :, :queries] = jnp.where(low, both, 0.0).astype(jnp.bfloat16)
        qs[h, :, queries:] = jnp.where(low, 0.0, both).astype(jnp.bfloat16)
        return carry

    lax.fori_loop(0, pairs, split_pair, 0)

    hops, mates = [[], []], [[], []]
    skew = 2
    for time in range(half + 2 + skew):
        for chunk in range(2):
            step = time - skew * chunk
            if step < 0 or step > half + 1:
                continue
            if step == 0:
                local[chunk].wait()
                for copy in arrivals[chunk]:
                    copy.wait_recv()
                for index in range(tiles_ref.shape[0]):
                    picked = got[chunk][tiles_ref[index]]
                    kv[core, index * share_rows:(index + 1) * share_rows, columns_of[chunk]] = picked
                hops[chunk] = [hop(1, side, chunk) for side in range(2)]
                mates[chunk] = [share(0, 0, chunk)]
                sent += hops[chunk] + mates[chunk]
                continue
            for copy in hops[chunk]:
                copy.wait_recv()
            hops[chunk] = [hop(step + 1, side, chunk) for side in range(2)] if step < half else []
            shared = [share(step, side, chunk) for side in range(2 if step < half else 1)] if step <= half else []
            sent += hops[chunk] + shared
            for copy in mates[chunk]:
                copy.wait_recv()
            mates[chunk] = shared
            length = 2 * rows if 0 < step - 1 < half else rows
            compute(slot(step - 1), length, step == 1, chunk * (pairs // 2), (chunk + 1) * (pairs // 2))

    def finish(h, carry):
        columns = pl.ds(pl.multiple_of(h * LANES, LANES), LANES)
        done = [acc[h, odd, :HALF] / acc[h, odd, HALF:HALF + 1] for odd in range(2)]
        o_ref[:, columns] = jnp.transpose(jnp.concatenate(done, axis=0)).astype(jnp.bfloat16)
        return carry

    lax.fori_loop(0, pairs, finish, 0)
    for copy in sent:
        copy.wait_send()


def attend(keys, values, queries, tiles, n):
    rows, width = queries.shape
    pairs = width // LANES
    half = n // 4
    vmem = pl.BlockSpec(memory_space=pltpu.VMEM)
    share_rows = keys.shape[2]
    hop_sems = pltpu.SemaphoreType.DMA((2, half + 1, 2))
    return pl.pallas_call(
        functools.partial(attend_kernel, n),
        out_shape=jax.ShapeDtypeStruct((rows, width), jnp.bfloat16),
        in_specs=[pl.BlockSpec(memory_space=pltpu.SMEM), pl.BlockSpec(memory_space=pl.ANY), pl.BlockSpec(memory_space=pl.ANY), vmem],
        out_specs=vmem,
        scratch_shapes=[
            [pltpu.VMEM((n * TILES_DEV, share_rows, width // 2), jnp.bfloat16)] * 2,
            pltpu.VMEM((2, tiles.shape[0] * TILE, width), jnp.bfloat16),
            pltpu.VMEM((pairs, LANES, 2 * rows), jnp.bfloat16),
            pltpu.VMEM((pairs, 2, 1, rows), jnp.float32),
            pltpu.VMEM((pairs, 2, HALF + ONES, rows), jnp.float32),
            [pltpu.SemaphoreType.DMA((2, n)), pltpu.SemaphoreType.DMA((2, n)), hop_sems, hop_sems, hop_sems, hop_sems],
        ],
        compiler_params=pltpu.CompilerParams(
            collective_id=0, has_side_effects=True, vmem_limit_bytes=52 * 1024 * 1024
        ),
    )(tiles, keys, values, queries)


def body(hidden, query_rows, key_rows, value_rows, out_weight, masked_tiles):
    n = lax.axis_size("seq")
    device = lax.axis_index("seq")
    tokens, width = key_rows.shape

    def by_chip(field):
        return field.reshape(TILES_DEV, n // 2, 2 * TILE // n, width)

    attended = attend(by_chip(key_rows), by_chip(value_rows), query_rows, masked_tiles, n)
    here = device * TILES_DEV + jnp.arange(tokens, dtype=jnp.int32) // TILE
    masked = jnp.any(here[:, None] == masked_tiles[None, :], axis=1)
    residual = jnp.dot(attended, out_weight, preferred_element_type=jnp.float32).astype(jnp.bfloat16)
    residual = jnp.where(masked[:, None], residual, jnp.zeros_like(residual))
    painted = hidden.astype(jnp.float32) + residual.astype(jnp.float32)
    return painted.astype(jnp.bfloat16)


def solution(mesh):
    placed = (
        P(("groups", "seq"), None),
        P(("groups", "seq"), None),
        P(("groups", "seq"), None),
        P(("groups", "seq"), None),
        P(),
        P("groups"),
    )
    return jax.shard_map(
        body, mesh=mesh, in_specs=placed, out_specs=P(("groups", "seq"), None), check_vma=False
    )
```

```python
import functools
import math

import jax
import jax.numpy as jnp
from jax import lax
from jax.experimental import pallas as pl
from jax.experimental.pallas import tpu as pltpu
from jax.sharding import PartitionSpec as P

HEADS = 24
TILE = 128
TILES_DEV = 3
LANES = 128
HALF = 64
ONES = 16
MESH = pl.DeviceIdType.MESH


def ring_device(place, chips, core):
    place = lax.rem(place + chips, chips)
    if chips == 8:
        chip = jnp.where(place < 4, 2 * place, 2 * (7 - place) + 1)
    else:
        chip = place
    return 2 * chip + core


def ring_place(device, chips):
    chip = device // 2
    if chips == 8:
        return jnp.where(lax.rem(chip, 2) == 0, chip // 2, 7 - chip // 2)
    return chip


def attend_kernel(n, tiles_ref, keys_ref, values_ref, q_ref, o_ref, got, kv, qs, best, acc, sems):
    deal_send, deal_recv, hop_send, hop_recv, mate_send, mate_recv = sems
    device = lax.axis_index("seq")
    core = lax.rem(device, 2)
    chips = n // 2
    half = chips // 2
    place = ring_place(device, chips)
    sides = (ring_device(place + 1, chips, core), ring_device(place - 1, chips, core))
    mate = device + 1 - 2 * core
    queries, width = q_ref.shape
    pairs = width // LANES
    share_rows = keys_ref.shape[2]
    rows = kv.shape[1] // chips
    part = rows // 2

    barrier = pltpu.get_barrier_semaphore()
    for away in range(1, n):
        other = lax.rem(device + away, n)
        pl.semaphore_signal(barrier, inc=1, device_id={"seq": other}, device_id_type=MESH)
    pl.semaphore_wait(barrier, n - 1)

    def slot(step):
        return 0 if step == 0 else rows + (step - 1) * 2 * rows

    columns_of = [pl.ds(chunk * (width // 2), width // 2) for chunk in range(2)]

    def region(step, side, chunk, last=False):
        base = slot(step) + (rows * side if 0 < step < half else 0)
        start, size = (side * part, part) if last else (0, rows)
        return kv.at[core, pl.ds(base + start, size), columns_of[chunk]]

    def remote(src, dst, send, recv, target):
        copy = pltpu.make_async_remote_copy(
            src_ref=src, dst_ref=dst, send_sem=send, recv_sem=recv,
            device_id={"seq": target}, device_id_type=MESH)
        copy.start()
        return copy

    def hop(step, side, chunk):
        last = step == half
        return remote(region(step - 1, side, chunk, last), region(step, side, chunk, last), hop_send.at[side, step, chunk],
                      hop_recv.at[side, step, chunk], sides[side])

    def share(step, side, chunk):
        block = region(step, side, chunk)
        return remote(block, block, mate_send.at[side, step, chunk], mate_recv.at[side, step, chunk], mate)

    def compute(start, length, first, low_pair, high_pair):
        def one_pair(h, carry):
            columns = pl.ds(pl.multiple_of(h * LANES, LANES), LANES)
            keys = kv[0, start:start + length, columns]
            values = jnp.transpose(kv[1, start:start + length, columns])
            ones = jnp.ones((ONES, length), jnp.bfloat16)
            both = jnp.dot(keys, qs[h], preferred_element_type=jnp.float32)
            for odd in range(2):
                mine = values[odd * HALF:(odd + 1) * HALF]
                value_one = jnp.concatenate([mine, ones], axis=0)
                scores = both[:, odd * queries:(odd + 1) * queries]
                top = jnp.max(scores, axis=0, keepdims=True)
                if first:
                    weights = jnp.exp(scores - top)
                    acc[h, odd] = jnp.dot(value_one, weights.astype(jnp.bfloat16), preferred_element_type=jnp.float32)
                    best[h, odd] = top
                else:
                    old = best[h, odd]
                    new = jnp.maximum(old, top)
                    weights = jnp.exp(scores - new)
                    more = jnp.dot(value_one, weights.astype(jnp.bfloat16), preferred_element_type=jnp.float32)
                    acc[h, odd] = acc[h, odd] * jnp.exp(old - new) + more
                    best[h, odd] = new
            return carry

        lax.fori_loop(low_pair, high_pair, one_pair, 0, unroll=2)

    def landing(source, chunk):
        return got[chunk].at[pl.ds(TILES_DEV * source, TILES_DEV)]

    chip = device // 2
    fields = (keys_ref, values_ref)
    sent, arrivals, local = [], [[], []], []

    def to_mate(chunk, kept):
        source = fields[1 - kept].at[:, chip, :, columns_of[chunk]]
        return pltpu.make_async_remote_copy(
            src_ref=source, dst_ref=landing(device, chunk), send_sem=deal_send.at[chunk, 1],
            recv_sem=deal_recv.at[chunk, 1], device_id={"seq": mate}, device_id_type=MESH)

    def to_self(chunk, kept):
        source = fields[kept].at[:, chip, :, columns_of[chunk]]
        return pltpu.make_async_copy(source, landing(device, chunk), deal_send.at[chunk, 0])

    def deal(chunk):
        for away in range(chips - 1, 0, -1):
            other = lax.rem(chip + away, chips)
            for wanted in range(2):
                source = fields[wanted].at[:, other, :, columns_of[chunk]]
                send = deal_send.at[chunk, 2 * away + wanted]
                sent.append(remote(source, landing(device, chunk), send, deal_recv.at[chunk, 2 * away + core],
                                   2 * other + wanted))
                arrivals[chunk].append(pltpu.make_async_remote_copy(
                    src_ref=source, dst_ref=landing(device, chunk), send_sem=send,
                    recv_sem=deal_recv.at[chunk, 2 * away + wanted],
                    device_id={"seq": 2 * other + wanted}, device_id_type=MESH))
        for kept in range(2):
            @pl.when(core == kept)
            def _():
                to_mate(chunk, kept).start()
                to_self(chunk, kept).start()
        arrivals[chunk].append(to_mate(chunk, 0))
        sent.append(arrivals[chunk][-1])
        local.append(to_self(chunk, 0))

    deal(0)
    deal(1)

    scale = 1.0 / math.sqrt(width // HEADS)

    def split_pair(h, carry):
        columns = pl.ds(pl.multiple_of(h * LANES, LANES), LANES)
        both = jnp.transpose(q_ref[:, columns].astype(jnp.float32) * scale)
        low = lax.broadcasted_iota(jnp.int32, (LANES, 1), 0) < HALF
        qs[h, :, :queries] = jnp.where(low, both, 0.0).astype(jnp.bfloat16)
        qs[h, :, queries:] = jnp.where(low, 0.0, both).astype(jnp.bfloat16)
        return carry

    lax.fori_loop(0, pairs, split_pair, 0)

    hops, mates = [[], []], [[], []]
    skew = 1
    for time in range(half + 2 + skew):
        for chunk in range(2):
            step = time - skew * chunk
            if step < 0 or step > half + 1:
                continue
            if step == 0:
                local[chunk].wait()
                for copy in arrivals[chunk]:
                    copy.wait_recv()
                for index in range(tiles_ref.shape[0]):
                    picked = got[chunk][tiles_ref[index]]
                    kv[core, index * share_rows:(index + 1) * share_rows, columns_of[chunk]] = picked
                hops[chunk] = [hop(1, side, chunk) for side in range(2)]
                mates[chunk] = [share(0, 0, chunk)]
                sent += hops[chunk] + mates[chunk]
                continue
            for copy in hops[chunk]:
                copy.wait_recv()
            hops[chunk] = [hop(step + 1, side, chunk) for side in range(2)] if step < half else []
            shared = [share(step, side, chunk) for side in range(2 if step < half else 1)] if step <= half else []
            sent += hops[chunk] + shared
            for copy in mates[chunk]:
                copy.wait_recv()
            mates[chunk] = shared
            length = 2 * rows if 0 < step - 1 < half else rows
            compute(slot(step - 1), length, step == 1, chunk * (pairs // 2), (chunk + 1) * (pairs // 2))

    def finish(h, carry):
        columns = pl.ds(pl.multiple_of(h * LANES, LANES), LANES)
        done = [acc[h, odd, :HALF] / acc[h, odd, HALF:HALF + 1] for odd in range(2)]
        o_ref[:, columns] = jnp.transpose(jnp.concatenate(done, axis=0)).astype(jnp.bfloat16)
        return carry

    lax.fori_loop(0, pairs, finish, 0)
    for copy in sent:
        copy.wait_send()


def attend(keys, values, queries, tiles, n):
    rows, width = queries.shape
    pairs = width // LANES
    half = n // 4
    vmem = pl.BlockSpec(memory_space=pltpu.VMEM)
    share_rows = keys.shape[2]
    hop_sems = pltpu.SemaphoreType.DMA((2, half + 1, 2))
    return pl.pallas_call(
        functools.partial(attend_kernel, n),
        out_shape=jax.ShapeDtypeStruct((rows, width), jnp.bfloat16),
        in_specs=[pl.BlockSpec(memory_space=pltpu.SMEM), pl.BlockSpec(memory_space=pl.ANY), pl.BlockSpec(memory_space=pl.ANY), vmem],
        out_specs=vmem,
        scratch_shapes=[
            [pltpu.VMEM((n * TILES_DEV, share_rows, width // 2), jnp.bfloat16)] * 2,
            pltpu.VMEM((2, tiles.shape[0] * TILE, width), jnp.bfloat16),
            pltpu.VMEM((pairs, LANES, 2 * rows), jnp.bfloat16),
            pltpu.VMEM((pairs, 2, 1, rows), jnp.float32),
            pltpu.VMEM((pairs, 2, HALF + ONES, rows), jnp.float32),
            [pltpu.SemaphoreType.DMA((2, n)), pltpu.SemaphoreType.DMA((2, n)), hop_sems, hop_sems, hop_sems, hop_sems],
        ],
        compiler_params=pltpu.CompilerParams(
            collective_id=0, has_side_effects=True, vmem_limit_bytes=52 * 1024 * 1024
        ),
    )(tiles, keys, values, queries)


def body(hidden, query_rows, key_rows, value_rows, out_weight, masked_tiles):
    n = lax.axis_size("seq")
    device = lax.axis_index("seq")
    tokens, width = key_rows.shape

    def by_chip(field):
        return field.reshape(TILES_DEV, n // 2, 2 * TILE // n, width)

    attended = attend(by_chip(key_rows), by_chip(value_rows), query_rows, masked_tiles, n)
    here = device * TILES_DEV + jnp.arange(tokens, dtype=jnp.int32) // TILE
    masked = jnp.any(here[:, None] == masked_tiles[None, :], axis=1)
    residual = jnp.dot(attended, out_weight, preferred_element_type=jnp.float32).astype(jnp.bfloat16)
    residual = jnp.where(masked[:, None], residual, jnp.zeros_like(residual))
    painted = hidden.astype(jnp.float32) + residual.astype(jnp.float32)
    return painted.astype(jnp.bfloat16)


def solution(mesh):
    placed = (
        P(("groups", "seq"), None),
        P(("groups", "seq"), None),
        P(("groups", "seq"), None),
        P(("groups", "seq"), None),
        P(),
        P("groups"),
    )
    return jax.shard_map(
        body, mesh=mesh, in_specs=placed, out_specs=P(("groups", "seq"), None), check_vma=False
    )
```
